32 devices in a mesh: dp: 4 (over z), mp: 8 (over y, x, core).
Axes of the slice: x: 2, y: 2, z: 4, core: 2. Of those that a mesh axis runs over, the one named last changes fastest.
Arguments:
- gradient: bfloat16 [4, 8192, 8192], P('dp', 'mp'), may hold values from -6 to 6
- error: bfloat16 [4, 8192, 8192], P('dp', 'mp'), may hold values from -4 to 4
- query: bfloat16 [8192, 256], P('mp'), may hold values from -0.0625 to 0.0625
Outputs:
- factor: float32 [8192, 256], P('mp')
- new_error: bfloat16 [4, 8192, 8192], P('dp', 'mp')
The draws below stay inside these ranges and needn't reach their ends.
All inputs are finite; a program needn't handle non-finite values.
Results may differ from the reference program's by a relative error of at most 0.013.
Values may be sent and summed in bfloat16 or wider, within the bound.
A program may use at most 128 MiB of HBM per device.

```python
import jax
import jax.numpy as jnp
from jax import lax

ROWS = 8192
COLS = 8192
RANK = 256
REPLICAS = 4
N_DP = 4


def levels(own_key, extent, shards, least, top_value):
    level, own = 1.0, jax.random.fold_in(own_key, 6)
    for position, blocks in shards:
        heights = jnp.exp(jax.random.uniform(jax.random.fold_in(own, position), (blocks,), jnp.float32, least / len(shards), top_value / len(shards)))
        level = level * jnp.repeat(heights, extent[position] // blocks).reshape([-1 if axis == position else 1 for axis in range(len(extent))])
    return level


def noise(key, shape, width, reach, cuts=(), held_as=jnp.bfloat16):
    factor_of = levels(key, shape, cuts, -0.22, 0.18) if cuts else 1.0
    result = jax.random.normal(key, shape, jnp.float32) * width * factor_of
    return jnp.minimum(jnp.maximum(result, -reach), reach).astype(held_as)


def setup_inputs(seed: int = 0) -> dict:
    seeds = jax.random.split(jax.random.key(seed), 4)
    return {
        "gradient": noise(seeds[0], (REPLICAS, ROWS, COLS), 1.0, 6.0, ((0, 4), (1, 8))),
        "error": noise(seeds[1], (REPLICAS, ROWS, COLS), 0.5, 4.0, ((0, 4), (1, 8))),
        "query": noise(seeds[2], (COLS, RANK), COLS ** -0.5, 0.0625, ((0, 8),)),
    }


def reference(gradient, error, query):
    adjusted = (gradient.astype(jnp.float32) + error.astype(jnp.float32)).astype(jnp.bfloat16)
    projections = lax.map(lambda block: jnp.dot(block.astype(jnp.float32), query.astype(jnp.float32), preferred_element_type=jnp.float32), adjusted)
    summed = jnp.sum(projections, axis=0)
    gram = jnp.dot(summed.T, summed, precision=lax.Precision.HIGHEST)
    lower = jnp.linalg.cholesky(gram)
    basis = lax.linalg.triangular_solve(lower, summed, left_side=False, lower=True, transpose_a=True).astype(jnp.bfloat16)
    terms = lax.map(lambda block: lax.dot_general(block.astype(jnp.float32), basis.astype(jnp.float32), (((0,), (0,)), ((), ())), preferred_element_type=jnp.float32), adjusted)
    factor = jnp.sum(terms, axis=0) / N_DP
    factor_half = factor.astype(jnp.bfloat16)
    approx = lax.dot_general(basis.astype(jnp.float32), factor_half.astype(jnp.float32), (((1,), (1,)), ((), ())), preferred_element_type=jnp.float32)
    new_error = (adjusted.astype(jnp.float32) - approx[None]).astype(jnp.bfloat16)
    return (factor, new_error)
```

```python
import functools

import jax
import jax.numpy as jnp
from jax import lax
from jax.experimental import pallas as pl
from jax.experimental.pallas import tpu as pltpu
from jax.sharding import PartitionSpec as P

F32, BF16 = jnp.float32, jnp.bfloat16
PANEL, GROUP = 32, 4


def dot_hi(a, b, dims):
    return lax.dot_general(a, b, (dims, ((), ())), precision=lax.Precision.HIGHEST, preferred_element_type=F32)


def inverse_of_panel(block):
    size = block.shape[0]
    eye = (lax.broadcasted_iota(jnp.int32, (size, size), 0) == lax.broadcasted_iota(jnp.int32, (size, size), 1)).astype(F32)
    work = jnp.concatenate([block, eye, jnp.zeros((size, 128 - 2 * size), F32)], axis=1)
    row_id = lax.broadcasted_iota(jnp.int32, (size, 128), 0)
    scale = jnp.zeros((size, 128), F32)
    for start in range(0, size, GROUP):
        ids = range(start, start + GROUP)
        cols = [jnp.broadcast_to(work[:, k:k + 1], (size, 128)) for k in ids]
        rows = [work[k:k + 1, :] for k in ids]
        pivots = [[jnp.broadcast_to(work[k:k + 1, l:l + 1], (1, 128)) for l in ids] for k in ids]
        for j, k in enumerate(ids):
            recip = 1.0 / pivots[j][j]
            scale = jnp.where(row_id == k, pivots[j][j], scale)
            work = work - jnp.where(row_id > k, cols[j] * recip, 0.0) * rows[j]
            for i in range(j + 1, GROUP):
                ratio = pivots[j][i] * recip
                cols[i] = cols[i] - cols[j] * ratio
                rows[i] = rows[i] - rows[j] * ratio
                for l in range(i, GROUP):
                    pivots[i][l] = pivots[i][l] - ratio * pivots[j][l]
    return (work * lax.rsqrt(scale))[:, size:2 * size]


def inverse_kernel(gram_ref, out_ref, work):
    rank = gram_ref.shape[0]
    work[:, :rank] = gram_ref[...]
    work[:, rank:] = (lax.broadcasted_iota(jnp.int32, (rank, rank), 0) == lax.broadcasted_iota(jnp.int32, (rank, rank), 1)).astype(F32)
    for start in range(0, rank, PANEL):
        stop = start + PANEL
        inverse = inverse_of_panel(work[start:stop, start:stop])
        panel = dot_hi(inverse, work[start:stop, :], ((1,), (0,)))
        out_ref[start:stop, :] = panel[:, rank:]
        if stop < rank:
            work[stop:, :] = work[stop:, :] - dot_hi(panel[:, stop:rank], panel, ((0,), (0,)))


def inverse_factor(gram):
    rank = gram.shape[0]
    return pl.pallas_call(
        inverse_kernel,
        out_shape=jax.ShapeDtypeStruct((rank, rank), F32),
        in_specs=[pl.BlockSpec(memory_space=pltpu.VMEM)],
        out_specs=pl.BlockSpec(memory_space=pltpu.VMEM),
        scratch_shapes=[pltpu.VMEM((rank, 2 * rank), F32)],
        compiler_params=pltpu.CompilerParams(vmem_limit_bytes=16 * 2**20),
    )(gram)


def swap(value, step):
    axis, bit = step
    return lax.ppermute(value, axis, [(i, i ^ bit) for i in range(lax.axis_size(axis))])


def upper(step):
    return (lax.axis_index(step[0]) // step[1]) % 2


def bits(axis):
    return [(axis, 1 << b) for b in range(lax.axis_size(axis).bit_length() - 1)]


def scatter_sum(value, steps):
    for step in steps:
        half, mine = value.shape[0] // 2, upper(step)
        sent = lax.dynamic_slice_in_dim(value, (1 - mine) * half, half, 0).astype(BF16)
        got = swap(sent, step)
        value = lax.dynamic_slice_in_dim(value, mine * half, half, 0).astype(F32) + got.astype(F32)
    return value


def joined(value, step, axis):
    got, mine = swap(value, step), upper(step) == 1
    return jnp.concatenate([jnp.where(mine, got, value), jnp.where(mine, value, got)], axis=axis)


def gather(value, steps):
    for step in reversed(steps):
        value = joined(value, step, 0)
    return value


def gather_blocks(value, order, steps):
    value = value.reshape((1,) * len(steps) + value.shape)
    for place in order:
        value = joined(value, steps[place], len(steps) - 1 - place)
    return value.reshape((-1,) + value.shape[len(steps):])


def shards(gradient, error, query):
    replicas = lax.axis_size("dp")
    mp, dp = bits("mp"), bits("dp")
    adjusted = (gradient[0].astype(F32) + error[0].astype(F32)).astype(BF16)
    half = query.shape[0] // 2
    forth = list(range(1, len(mp))) + [0]
    back = list(range(len(mp) - 1, 0, -1)) + [0]
    whole = jnp.concatenate(
        [gather_blocks(query[:half], forth, mp), gather_blocks(query[half:], back, mp)], axis=1
    ).reshape(-1, query.shape[1])
    projection = jnp.dot(adjusted, whole, preferred_element_type=F32)
    summed = gather(scatter_sum(projection, dp).astype(BF16), dp)
    gram = lax.dot_general(summed, summed, (((0,), (0,)), ((), ())), preferred_element_type=F32)
    for step in mp:
        gram = gram + swap(gram, step)
    inverse = inverse_factor(gram)
    basis = dot_hi(summed.astype(F32), inverse, ((1,), (1,))).astype(BF16)
    term = lax.dot_general(adjusted, basis, (((0,), (0,)), ((), ())), preferred_element_type=F32)
    first = scatter_sum(term, mp[:1])
    cut = first.shape[0] // 2
    one, two = mp[1:] + dp, mp[:0:-1] + dp
    parts = [(first[:cut], one), (first[cut:], two)]
    gathered = [
        gather((scatter_sum(part, steps) / replicas).astype(BF16), steps) for part, steps in parts
    ]
    factor_half = gather(jnp.concatenate(gathered, axis=0), mp[:1])
    own = lax.dynamic_slice_in_dim(
        factor_half, lax.axis_index("mp") * query.shape[0], query.shape[0], 0
    ).astype(F32)
    approx = lax.dot_general(basis, factor_half, (((1,), (1,)), ((), ())), preferred_element_type=F32)
    new_error = (adjusted.astype(F32) - approx).astype(BF16)
    return (own, new_error[None])


def solution(mesh):
    in_specs = (P("dp", "mp", None), P("dp", "mp", None), P("mp", None))
    out_specs = (P("mp", None), P("dp", "mp", None))
    return jax.shard_map(shards, mesh=mesh, in_specs=in_specs, out_specs=out_specs, check_vma=False)
```

```python
import functools

import jax
import jax.numpy as jnp
from jax import lax
from jax.experimental import pallas as pl
from jax.experimental.pallas import tpu as pltpu
from jax.sharding import PartitionSpec as P

F32, BF16 = jnp.float32, jnp.bfloat16
PANEL, GROUP, TILE = 32, 4, 512


def dot_hi(a, b, dims):
    return lax.dot_general(a, b, (dims, ((), ())), precision=lax.Precision.HIGHEST, preferred_element_type=F32)


def inverse_of_panel(block):
    size = block.shape[0]
    eye = (lax.broadcasted_iota(jnp.int32, (size, size), 0) == lax.broadcasted_iota(jnp.int32, (size, size), 1)).astype(F32)
    work = jnp.concatenate([block, eye, jnp.zeros((size, 128 - 2 * size), F32)], axis=1)
    row_id = lax.broadcasted_iota(jnp.int32, (size, 128), 0)
    scale = jnp.zeros((size, 128), F32)
    for start in range(0, size, GROUP):
        ids = range(start, start + GROUP)
        cols = [jnp.broadcast_to(work[:, k:k + 1], (size, 128)) for k in ids]
        rows = [work[k:k + 1, :] for k in ids]
        pivots = [[jnp.broadcast_to(work[k:k + 1, l:l + 1], (1, 128)) for l in ids] for k in ids]
        for j, k in enumerate(ids):
            recip = 1.0 / pivots[j][j]
            scale = jnp.where(row_id == k, pivots[j][j], scale)
            work = work - jnp.where(row_id > k, cols[j] * recip, 0.0) * rows[j]
            for i in range(j + 1, GROUP):
                ratio = pivots[j][i] * recip
                cols[i] = cols[i] - cols[j] * ratio
                rows[i] = rows[i] - rows[j] * ratio
                for l in range(i, GROUP):
                    pivots[i][l] = pivots[i][l] - ratio * pivots[j][l]
    return (work * lax.rsqrt(scale))[:, size:2 * size]


def inverse_kernel(gram_ref, out_ref, work):
    rank = gram_ref.shape[0]
    work[:, :rank] = gram_ref[...]
    work[:, rank:] = (lax.broadcasted_iota(jnp.int32, (rank, rank), 0) == lax.broadcasted_iota(jnp.int32, (rank, rank), 1)).astype(F32)
    for start in range(0, rank, PANEL):
        stop = start + PANEL
        inverse = inverse_of_panel(work[start:stop, start:stop])
        panel = dot_hi(inverse, work[start:stop, :], ((1,), (0,)))
        out_ref[start:stop, :] = panel[:, rank:]
        if stop < rank:
            work[stop:, :] = work[stop:, :] - dot_hi(panel[:, stop:rank], panel, ((0,), (0,)))


def inverse_factor(gram):
    rank = gram.shape[0]
    return pl.pallas_call(
        inverse_kernel,
        out_shape=jax.ShapeDtypeStruct((rank, rank), F32),
        in_specs=[pl.BlockSpec(memory_space=pltpu.VMEM)],
        out_specs=pl.BlockSpec(memory_space=pltpu.VMEM),
        scratch_shapes=[pltpu.VMEM((rank, 2 * rank), F32)],
        compiler_params=pltpu.CompilerParams(vmem_limit_bytes=16 * 2**20),
    )(gram)


def term_kernel(left_ref, adjusted_ref, out_ref):
    product = jnp.dot(left_ref[...], adjusted_ref[...], preferred_element_type=F32)
    out_ref[...] = product.T


def term_of(adjusted, basis):
    rows, cols = adjusted.shape
    rank = basis.shape[1]
    return pl.pallas_call(
        term_kernel,
        grid=(cols // TILE,),
        out_shape=jax.ShapeDtypeStruct((cols, rank), F32),
        in_specs=[pl.BlockSpec((rank, rows), lambda j: (0, 0)), pl.BlockSpec((rows, TILE), lambda j: (0, j))],
        out_specs=pl.BlockSpec((TILE, rank), lambda j: (j, 0)),
        cost_estimate=pl.CostEstimate(flops=2 * rows * cols * rank, bytes_accessed=2 * rows * cols + 4 * cols * rank, transcendentals=0),
        compiler_params=pltpu.CompilerParams(vmem_limit_bytes=16 * 2**20),
    )(basis.T, adjusted)


def residual_kernel(tiles, mine_ref, basis_ref, held_ref, got_ref, adjusted_ref, out_ref):
    is_held = (pl.program_id(0) // tiles) == mine_ref[0]
    factor = jnp.where(is_held, held_ref[...].astype(F32), got_ref[...].astype(F32)).astype(BF16)
    approx = lax.dot_general(basis_ref[...], factor, (((1,), (1,)), ((), ())), preferred_element_type=F32)
    out_ref[...] = (adjusted_ref[...].astype(F32) - approx).astype(BF16)


def residual(adjusted, basis, held, got, mine):
    rows, cols = adjusted.shape
    rank = basis.shape[1]
    tiles = cols // 2 // TILE
    half = pl.BlockSpec((TILE, rank), lambda j: (j % tiles, 0))
    wide = pl.BlockSpec((rows, TILE), lambda j: (0, j))
    return pl.pallas_call(
        functools.partial(residual_kernel, tiles),
        grid=(2 * tiles,),
        out_shape=jax.ShapeDtypeStruct((rows, cols), BF16),
        in_specs=[pl.BlockSpec(memory_space=pltpu.SMEM), pl.BlockSpec((rows, rank), lambda j: (0, 0)), half, half, wide],
        out_specs=wide,
        cost_estimate=pl.CostEstimate(flops=2 * rows * cols * rank, bytes_accessed=4 * rows * cols, transcendentals=0),
        compiler_params=pltpu.CompilerParams(vmem_limit_bytes=16 * 2**20),
    )(mine.reshape(1).astype(jnp.int32), basis, held, got, adjusted)


def swap(value, step):
    axis, bit = step
    return lax.ppermute(value, axis, [(i, i ^ bit) for i in range(lax.axis_size(axis))])


def upper(step):
    return (lax.axis_index(step[0]) // step[1]) % 2


def bits(axis):
    return [(axis, 1 << b) for b in range(lax.axis_size(axis).bit_length() - 1)]


def scatter_sum(value, steps):
    for step in steps:
        half, mine = value.shape[0] // 2, upper(step)
        sent = lax.dynamic_slice_in_dim(value, (1 - mine) * half, half, 0).astype(BF16)
        got = swap(sent, step)
        value = lax.dynamic_slice_in_dim(value, mine * half, half, 0).astype(F32) + got.astype(F32)
    return value


def joined(value, step, axis):
    got, mine = swap(value, step), upper(step) == 1
    return jnp.concatenate([jnp.where(mine, got, value), jnp.where(mine, value, got)], axis=axis)


def gather(value, steps):
    for step in reversed(steps):
        value = joined(value, step, 0)
    return value


def gather_blocks(value, order, steps):
    for place in order:
        value = joined(value, steps[place], len(steps) - 1 - place)
    return value


def shards(gradient, error, query):
    replicas = lax.axis_size("dp")
    mp, dp = bits("mp"), bits("dp")
    adjusted = (gradient[0].astype(F32) + error[0].astype(F32)).astype(BF16)
    half, rank = query.shape[0] // 2, query.shape[1]
    lead = (1,) * len(mp)
    forth, back = list(range(1, len(mp))), list(range(len(mp) - 1, 0, -1))
    halves = (
        gather_blocks(query[:half].reshape(lead + (half, rank)), forth, mp),
        gather_blocks(query[half:].reshape(lead + (half, rank)), back, mp),
    )
    adjusted, halves = lax.optimization_barrier((adjusted, halves))
    whole = jnp.concatenate([gather_blocks(side, [0], mp) for side in halves], axis=len(mp)).reshape(-1, rank)
    projection = jnp.dot(adjusted, whole, preferred_element_type=F32)
    summed = gather(scatter_sum(projection, dp).astype(BF16), dp)
    gram = lax.dot_general(summed, summed, (((0,), (0,)), ((), ())), preferred_element_type=F32)
    for step in mp:
        gram = gram + swap(gram, step)
    inverse = inverse_factor(gram)
    basis = dot_hi(summed.astype(F32), inverse, ((1,), (1,))).astype(BF16)
    term = term_of(adjusted, basis)
    first = scatter_sum(term, mp[:1])
    cut = first.shape[0] // 2
    one, two = mp[1:] + dp, mp[:0:-1] + dp
    parts = [(first[:cut], one), (first[cut:], two)]
    gathered = [
        gather((scatter_sum(part, steps) / replicas).astype(BF16), steps) for part, steps in parts
    ]
    held = jnp.concatenate(gathered, axis=0)
    got, mine = swap(held, mp[0]), upper(mp[0])
    start = lax.axis_index("mp") * query.shape[0]
    span = held.shape[0]
    own_rows = [lax.dynamic_slice_in_dim(side, start % span, query.shape[0], 0) for side in (held, got)]
    own = jnp.where(start // span == mine, own_rows[0], own_rows[1]).astype(F32)
    new_error = residual(adjusted, basis, held, got, mine)
    return (own, new_error[None])


def solution(mesh):
    in_specs = (P("dp", "mp", None), P("dp", "mp", None), P("mp", None))
    out_specs = (P("mp", None), P("dp", "mp", None))
    return jax.shard_map(shards, mesh=mesh, in_specs=in_specs, out_specs=out_specs, check_vma=False)
```

```python
import functools

import jax
import jax.numpy as jnp
from jax import lax
from jax.experimental import pallas as pl
from jax.experimental.pallas import tpu as pltpu
from jax.sharding import PartitionSpec as P

F32, BF16 = jnp.float32, jnp.bfloat16
PANEL, GROUP, TILE = 32, 4, 512


def dot_hi(a, b, dims):
    return lax.dot_general(a, b, (dims, ((), ())), precision=lax.Precision.HIGHEST, preferred_element_type=F32)


def inverse_of_panel(block):
    size = block.shape[0]
    eye = (lax.broadcasted_iota(jnp.int32, (size, size), 0) == lax.broadcasted_iota(jnp.int32, (size, size), 1)).astype(F32)
    work = jnp.concatenate([block, eye, jnp.zeros((size, 128 - 2 * size), F32)], axis=1)
    row_id = lax.broadcasted_iota(jnp.int32, (size, 128), 0)
    scale = jnp.zeros((size, 128), F32)
    for start in range(0, size, GROUP):
        ids = range(start, start + GROUP)
        cols = [jnp.broadcast_to(work[:, k:k + 1], (size, 128)) for k in ids]
        rows = [work[k:k + 1, :] for k in ids]
        pivots = [[jnp.broadcast_to(work[k:k + 1, l:l + 1], (1, 128)) for l in ids] for k in ids]
        for j, k in enumerate(ids):
            recip = 1.0 / pivots[j][j]
            scale = jnp.where(row_id == k, pivots[j][j], scale)
            work = work - jnp.where(row_id > k, cols[j] * recip, 0.0) * rows[j]
            for i in range(j + 1, GROUP):
                ratio = pivots[j][i] * recip
                cols[i] = cols[i] - cols[j] * ratio
                rows[i] = rows[i] - rows[j] * ratio
                for l in range(i, GROUP):
                    pivots[i][l] = pivots[i][l] - ratio * pivots[j][l]
    return (work * lax.rsqrt(scale))[:, size:2 * size]


def inverse_kernel(gram_ref, out_ref, work):
    rank = gram_ref.shape[0]
    work[:, :rank] = gram_ref[...]
    work[:, rank:] = (lax.broadcasted_iota(jnp.int32, (rank, rank), 0) == lax.broadcasted_iota(jnp.int32, (rank, rank), 1)).astype(F32)
    for start in range(0, rank, PANEL):
        stop = start + PANEL
        inverse = inverse_of_panel(work[start:stop, start:stop])
        panel = dot_hi(inverse, work[start:stop, :], ((1,), (0,)))
        out_ref[start:stop, :] = panel[:, rank:]
        if stop < rank:
            work[stop:, :] = work[stop:, :] - dot_hi(panel[:, stop:rank], panel, ((0,), (0,)))


def inverse_factor(gram):
    rank = gram.shape[0]
    return pl.pallas_call(
        inverse_kernel,
        out_shape=jax.ShapeDtypeStruct((rank, rank), F32),
        in_specs=[pl.BlockSpec(memory_space=pltpu.VMEM)],
        out_specs=pl.BlockSpec(memory_space=pltpu.VMEM),
        scratch_shapes=[pltpu.VMEM((rank, 2 * rank), F32)],
        compiler_params=pltpu.CompilerParams(vmem_limit_bytes=16 * 2**20),
    )(gram)


def term_kernel(left_ref, adjusted_ref, out_ref):
    product = jnp.dot(left_ref[...], adjusted_ref[...], preferred_element_type=F32)
    out_ref[...] = product.T


def term_of(adjusted, basis):
    rows, cols = adjusted.shape
    rank = basis.shape[1]
    return pl.pallas_call(
        term_kernel,
        grid=(cols // TILE,),
        out_shape=jax.ShapeDtypeStruct((cols, rank), F32),
        in_specs=[pl.BlockSpec((rank, rows), lambda j: (0, 0)), pl.BlockSpec((rows, TILE), lambda j: (0, j))],
        out_specs=pl.BlockSpec((TILE, rank), lambda j: (j, 0)),
        cost_estimate=pl.CostEstimate(flops=2 * rows * cols * rank, bytes_accessed=2 * rows * cols + 4 * cols * rank, transcendentals=0),
        compiler_params=pltpu.CompilerParams(vmem_limit_bytes=49 * 2**20),
    )(basis.T, adjusted)


def residual_kernel(tiles, mine_ref, basis_ref, held_ref, got_ref, adjusted_ref, out_ref):
    is_held = (pl.program_id(0) // tiles) == mine_ref[0]
    factor = jnp.where(is_held, held_ref[...].astype(F32), got_ref[...].astype(F32)).astype(BF16)
    approx = lax.dot_general(basis_ref[...], factor, (((1,), (1,)), ((), ())), preferred_element_type=F32)
    out_ref[...] = (adjusted_ref[...].astype(F32) - approx).astype(BF16)


def residual(adjusted, basis, held, got, mine):
    rows, cols = adjusted.shape
    rank = basis.shape[1]
    tiles = cols // 2 // TILE
    half = pl.BlockSpec((TILE, rank), lambda j: (j % tiles, 0))
    wide = pl.BlockSpec((rows, TILE), lambda j: (0, j))
    return pl.pallas_call(
        functools.partial(residual_kernel, tiles),
        grid=(2 * tiles,),
        out_shape=jax.ShapeDtypeStruct((rows, cols), BF16),
        in_specs=[pl.BlockSpec(memory_space=pltpu.SMEM), pl.BlockSpec((rows, rank), lambda j: (0, 0)), half, half, wide],
        out_specs=wide,
        cost_estimate=pl.CostEstimate(flops=2 * rows * cols * rank, bytes_accessed=4 * rows * cols, transcendentals=0),
        compiler_params=pltpu.CompilerParams(vmem_limit_bytes=49 * 2**20),
    )(mine.reshape(1).astype(jnp.int32), basis, held, got, adjusted)


def swap(value, step):
    axis, bit = step
    return lax.ppermute(value, axis, [(i, i ^ bit) for i in range(lax.axis_size(axis))])


def upper(step):
    return (lax.axis_index(step[0]) // step[1]) % 2


def bits(axis):
    return [(axis, 1 << b) for b in range(lax.axis_size(axis).bit_length() - 1)]


def scatter_sum(value, steps):
    for step in steps:
        half, mine = value.shape[0] // 2, upper(step)
        sent = lax.dynamic_slice_in_dim(value, (1 - mine) * half, half, 0).astype(BF16)
        got = swap(sent, step)
        value = lax.dynamic_slice_in_dim(value, mine * half, half, 0).astype(F32) + got.astype(F32)
    return value


def joined(value, step, axis):
    got, mine = swap(value, step), upper(step) == 1
    return jnp.concatenate([jnp.where(mine, got, value), jnp.where(mine, value, got)], axis=axis)


def gather(value, steps):
    for step in reversed(steps):
        value = joined(value, step, 0)
    return value


def gather_blocks(value, order, steps):
    for place in order:
        value = joined(value, steps[place], len(steps) - 1 - place)
    return value


def shards(gradient, error, query):
    replicas = lax.axis_size("dp")
    mp, dp = bits("mp"), bits("dp")
    adjusted = (gradient[0].astype(F32) + error[0].astype(F32)).astype(BF16)
    half, rank = query.shape[0] // 2, query.shape[1]
    lead = (1,) * len(mp)
    forth, back = list(range(1, len(mp))), list(range(len(mp) - 1, 0, -1))
    halves = (
        gather_blocks(query[:half].reshape(lead + (half, rank)), forth, mp),
        gather_blocks(query[half:].reshape(lead + (half, rank)), back, mp),
    )
    adjusted, halves = lax.optimization_barrier((adjusted, halves))
    whole = jnp.concatenate([gather_blocks(side, [0], mp) for side in halves], axis=len(mp)).reshape(-1, rank)
    projection = jnp.dot(adjusted, whole, preferred_element_type=F32)
    summed = gather(scatter_sum(projection, dp).astype(BF16), dp)
    gram = lax.dot_general(summed, summed, (((0,), (0,)), ((), ())), preferred_element_type=F32)
    for step in mp:
        gram = gram + swap(gram, step)
    inverse = inverse_factor(gram)
    basis = dot_hi(summed.astype(F32), inverse, ((1,), (1,))).astype(BF16)
    term = term_of(adjusted, basis)
    first = scatter_sum(term, mp[:1])
    cut = first.shape[0] // 2
    one, two = mp[1:] + dp, mp[:0:-1] + dp
    parts = [(first[:cut], one), (first[cut:], two)]
    gathered = [
        gather((scatter_sum(part, steps) / replicas).astype(BF16), steps) for part, steps in parts
    ]
    held = jnp.concatenate(gathered, axis=0)
    got, mine = swap(held, mp[0]), upper(mp[0])
    start = lax.axis_index("mp") * query.shape[0]
    span = held.shape[0]
    own_rows = [lax.dynamic_slice_in_dim(side, start % span, query.shape[0], 0) for side in (held, got)]
    own = jnp.where(start // span == mine, own_rows[0], own_rows[1]).astype(F32)
    new_error = residual(adjusted, basis, held, got, mine)
    return (own, new_error[None])


def solution(mesh):
    in_specs = (P("dp", "mp", None), P("dp", "mp", None), P("mp", None))
    out_specs = (P("mp", None), P("dp", "mp", None))
    return jax.shard_map(shards, mesh=mesh, in_specs=in_specs, out_specs=out_specs, check_vma=False)
```
